512 devices in a mesh: dp: 512 (over x, z, y, core).
Axes of the slice: x: 4, y: 4, z: 16, core: 2. Of those that a mesh axis runs over, the one named last changes fastest.
Arguments:
- image_feats: bfloat16 [65536, 640], P('dp'), may hold values from -6 to 6
- proj_head: bfloat16 [640, 1152], replicated, may hold values from -0.0068359375 to 0.0068359375
- rest_part: bfloat16 [65536, 1152], P('dp'), may hold values from -0.19921875 to 0.19921875
- text_embed: bfloat16 [65536, 1152], P('dp'), may hold values from -0.19921875 to 0.19921875
- logit_scale: float32 [1], replicated, may hold values from 5 to 15
- logit_bias: float32 [1], replicated, may hold values from -4 to -2
Outputs:
- grad_text: bfloat16 [65536, 1152], P('dp')
- grad_proj: bfloat16 [640, 1152], replicated
The draws below stay inside these ranges and needn't reach their ends.
All inputs are finite; a program needn't handle non-finite values.
Results may differ from the reference program's by a relative error of at most 0.0065.
Values may be sent and summed in bfloat16 or wider, within the bound.
A program may use at most 64 MiB of HBM per device.

```python
import jax
import jax.numpy as jnp
from jax import lax

D = 1152
F = 640
B_DEV = 128
STEPS = 8
TOKENS = 65536
N_DP = 512


def block_scale(stream_key, shape, pieces, low, largest):
    def one(axis_at, blocks):
        steps = jax.random.uniform(jax.random.fold_in(jax.random.fold_in(stream_key, 6), axis_at), (blocks,), jnp.float32, low / len(pieces), largest / len(pieces))
        return jnp.repeat(jnp.exp(steps), shape[axis_at] // blocks).reshape((-1,) + (1,) * (len(shape) - axis_at - 1))

    gain = one(*pieces[0])
    for cut in pieces[1:]:
        gain = gain * one(*cut)
    return gain


def gaussian(stream_key, shape, spread, bound, split=(), kind=jnp.bfloat16):
    result = jax.random.normal(stream_key, shape, jnp.float32) * spread
    if len(split) > 0:
        result = block_scale(stream_key, shape, split, -0.22, 0.18) * result
    return jnp.clip(result, min=-bound, max=bound).astype(kind)


def setup_inputs(seed: int = 0) -> dict:
    keys = jax.random.split(jax.random.key(seed), 7)
    image_feats = gaussian(keys[0], (TOKENS, F), 1.0, 6.0, ((0, 512),))
    proj_head = gaussian(keys[1], (F, D), (F * D) ** -0.5, 0.0068359375)
    rest_part = gaussian(keys[2], (TOKENS, D), 0.03, 0.19921875, ((0, 512),))
    text_embed = gaussian(keys[3], (TOKENS, D), 0.03, 0.19921875, ((0, 512),))
    logit_scale = jnp.clip(jax.random.uniform(keys[4], (1,), jnp.float32, 5.0, 15.0), 5.0, 15.0)
    logit_bias = jnp.clip(jax.random.uniform(keys[5], (1,), jnp.float32, -4.0, -2.0), -4.0, -2.0)
    return dict(image_feats=image_feats, proj_head=proj_head, rest_part=rest_part, text_embed=text_embed, logit_scale=logit_scale, logit_bias=logit_bias)


def unit_rows(raw):
    values = raw.astype(jnp.float32)
    squares = lax.optimization_barrier(jnp.sum(values * values, axis=-1, keepdims=True)) + 1e-06
    return (values, squares, (values / jnp.sqrt(squares)).astype(jnp.bfloat16))

def back_norm(values, squares, grads):
    inner = lax.optimization_barrier(jnp.sum(values * grads, axis=-1, keepdims=True))
    return (grads - values * inner / squares) / jnp.sqrt(squares)

def reference(image_feats, proj_head, rest_part, text_embed, logit_scale, logit_bias):
    scale = logit_scale[0]
    bias = logit_bias[0]
    y_full = jnp.dot(image_feats, proj_head, preferred_element_type=jnp.float32) + rest_part.astype(jnp.float32)
    y_vals, y_sq, image_unit = unit_rows(y_full)
    t_vals, t_sq, text_unit = unit_rows(text_embed)
    images = image_unit.reshape(N_DP, B_DEV, D)
    texts = text_unit.reshape(N_DP, B_DEV, D)
    images_f = images.astype(jnp.float32)
    grad_image = jnp.zeros((N_DP, B_DEV, D), jnp.float32)
    grad_texts = jnp.zeros((N_DP, B_DEV, D), jnp.float32)
    eye_mat = jnp.eye(B_DEV, dtype=jnp.float32)
    for step in range(STEPS):
        paired = jnp.roll(texts, step, axis=0).astype(jnp.float32)
        logits = scale * jnp.einsum('nid,njd->nij', images_f, paired) + bias
        if step == 0:
            label = 2.0 * eye_mat - 1.0
        else:
            label = -jnp.ones_like(eye_mat)
        coef = (-label * scale * jax.nn.sigmoid(-label * logits)).astype(jnp.bfloat16).astype(jnp.float32)
        grad_image = grad_image + jnp.einsum('nij,njd->nid', coef, paired)
        contrib = jnp.einsum('nij,nid->njd', coef, images_f)
        grad_texts = grad_texts + jnp.roll(contrib, -step, axis=0)
    grad_y = back_norm(y_vals, y_sq, grad_image.reshape(TOKENS, D)).astype(jnp.bfloat16)
    head = lax.dot_general(image_feats, grad_y, (((0,), (0,)), ((), ())), preferred_element_type=jnp.float32)
    grad_proj = (head / N_DP).astype(jnp.bfloat16)
    grad_text = back_norm(t_vals, t_sq, grad_texts.reshape(TOKENS, D)).astype(jnp.bfloat16)
    return (grad_text, grad_proj)
```

```python
import jax
import jax.numpy as jnp
from jax import lax
from jax.experimental import pallas as pl
from jax.experimental.pallas import tpu as pltpu
from jax.sharding import PartitionSpec as P

D = 1152
F = 640
B = 128
N = 512
MESH = pl.DeviceIdType.MESH
ROWS = 144
TILES = 45
OWN = 12
PAD = 48


def unit_rows(values):
    squares = jnp.sum(values * values, axis=-1, keepdims=True) + 1e-06
    return squares, (values / jnp.sqrt(squares)).astype(jnp.bfloat16)


def back_norm(values, squares, grads):
    inner = jnp.sum(values * grads, axis=-1, keepdims=True)
    return (grads - values * (inner / squares)) / jnp.sqrt(squares)


def coefficients(left, right, scale, bias, first):
    logits = bias + scale * lax.dot_general(
        left, right, (((1,), (1,)), ((), ())), preferred_element_type=jnp.float32
    )
    coef = scale * jax.nn.sigmoid(logits)
    if first:
        row = lax.broadcasted_iota(jnp.int32, logits.shape, 0)
        col = lax.broadcasted_iota(jnp.int32, logits.shape, 1)
        coef = jnp.where(row == col, -scale * jax.nn.sigmoid(-logits), coef)
    return coef.astype(jnp.bfloat16)


def kernel(
    feats_hbm, proj_hbm, rest_hbm, text_hbm, scale_ref, bias_ref,
    gt_ref, head_ref,
    texts, images, feats, proj, rest, text, yv, grad, gyt, gx, htf, ht, ry, sf, sb, rz, total,
    load, t_send, t_recv, i_send, i_recv, f_send, f_recv, x_send, x_recv, y_send, y_recv,
    z_send, z_recv, a_send, a_recv, b_send, b_recv, c_send, c_recv,
):
    me = lax.axis_index("dp")
    k = lax.rem(me, 2)
    y = lax.rem(lax.div(me, 2), 4)
    z = lax.rem(lax.div(me, 8), 16)
    x = lax.div(me, 128)
    sib = me + 1 - 2 * k
    block = 2 * x + k

    def ring(delta):
        return lax.rem(me + (delta + N), N)

    def at(ax, az, ay, ak):
        return ((ax * 16 + az) * 4 + ay) * 2 + ak

    def xs(i):
        return lax.rem(x + (i + 4), 4)

    def ys(i):
        return lax.rem(y + (i + 4), 4)

    def zs(i):
        return lax.rem(z + (i + 16), 16)

    def remote(src, dst, send, recv, device):
        return pltpu.make_async_remote_copy(
            src_ref=src, dst_ref=dst, send_sem=send, recv_sem=recv,
            device_id=(device,), device_id_type=MESH,
        )

    def start(*args):
        copy = remote(*args)
        copy.start()
        return copy

    def landed(dst, recv):
        remote(dst, dst, t_send.at[0], recv, sib).wait_recv()

    loads = [
        pltpu.make_async_copy(text_hbm, text, load.at[0]),
        pltpu.make_async_copy(feats_hbm, feats.at[block], load.at[1]),
        pltpu.make_async_copy(proj_hbm, proj, load.at[2]),
        pltpu.make_async_copy(rest_hbm, rest, load.at[3]),
    ]
    for copy in loads:
        copy.start()

    barrier = pltpu.get_barrier_semaphore()
    partners = [ring(d) for d in (2, -2, 4, -4, 6, -6)] + [sib, ring(-7 + 14 * k)]
    partners += [at(xs(i), z, y, kk) for i in (1, 2, 3) for kk in (0, 1)]
    partners += [at(x, zs(i), y, k) for i in range(1, 16)]
    for device in partners:
        pl.semaphore_signal(barrier, inc=1, device_id=(device,), device_id_type=MESH)

    scale = scale_ref[0]
    bias = bias_ref[0]

    loads[0].wait()
    t_sq, t_unit = unit_rows(text[...].astype(jnp.float32))
    texts[0] = t_unit
    pl.semaphore_wait(barrier, len(partners))

    t_copies = []
    for j in (1, 2, 3):
        t_copies.append(start(texts.at[0], texts.at[2 * j], t_send.at[j], t_recv.at[2 * j], ring(2 * j)))

    def odd_text(j):
        slot = lax.rem(2 * j + 9 - 2 * k, 8)
        device = ring(1 + 6 * k) if j == 0 else sib
        return start(texts.at[2 * j], texts.at[slot], t_send.at[4 + j], t_recv.at[slot], device)

    t_copies.append(odd_text(0))
    loads[1].wait()
    f_copies = []
    for i in (1, 2, 3):
        f_copies.append(start(feats.at[block], feats.at[block], f_send.at[i], f_recv.at[i], at(xs(i), z, y, k)))
    f_copies.append(start(feats.at[block], feats.at[block], f_send.at[4], f_recv.at[4], sib))

    loads[2].wait()
    loads[3].wait()
    y_full = jnp.dot(feats[block], proj[...], preferred_element_type=jnp.float32)
    y_full = y_full + rest[...].astype(jnp.float32)
    yv[...] = y_full
    y_sq, image_unit = unit_rows(y_full)
    images[0] = image_unit

    def image_side(j):
        pair = texts[2 * j : 2 * j + 2].reshape(2 * B, D)
        coef = coefficients(images[0], pair, scale, bias, j == 0)
        part = jnp.dot(coef, pair, preferred_element_type=jnp.float32)
        if j == 0:
            grad[...] = part
        else:
            grad[...] += part

    def text_side(j):
        pair = images[2 * j : 2 * j + 2].reshape(2 * B, D)
        coef = coefficients(texts[0], pair, scale, bias, j == 0)
        part = jnp.dot(coef, pair, preferred_element_type=jnp.float32)
        if j == 0:
            grad[...] = part
        else:
            grad[...] += part

    for i in (1, 2, 3):
        there = feats.at[2 * xs(-i) + k]
        landed(there, f_recv.at[i])
        f_copies.append(start(there, there, f_send.at[4 + i], f_recv.at[4 + i], sib))

    for j in (1, 2, 3):
        landed(texts.at[2 * j], t_recv.at[2 * j])
        t_copies.append(odd_text(j))
        landed(texts.at[2 * j - 1], t_recv.at[2 * j - 1])
        image_side(j - 1)
    for copy in t_copies[:3]:
        copy.wait_send()

    i_copies = []
    for j in (1, 2, 3):
        i_copies.append(start(images.at[0], images.at[2 * j], i_send.at[j], i_recv.at[2 * j], ring(-2 * j)))

    def odd_image(j):
        slot = lax.rem(2 * j + 7 + 2 * k, 8)
        device = ring(-7 + 6 * k) if j == 0 else sib
        return start(images.at[2 * j], images.at[slot], i_send.at[4 + j], i_recv.at[slot], device)

    i_copies.append(odd_image(0))

    landed(texts.at[7], t_recv.at[7])
    image_side(3)
    for copy in t_copies[3:]:
        copy.wait_send()

    grad_y = back_norm(yv[...], y_sq, grad[...]).astype(jnp.bfloat16)
    gyt[...] = jnp.transpose(grad_y.astype(jnp.float32)).astype(jnp.bfloat16).reshape(8, ROWS, B)

    x_copies = []
    for i in range(4):
        for kk in (0, 1):
            if i or kk:
                other = lax.rem(k + kk, 2)
                n = 2 * i + kk - 1
                x_copies.append(
                    start(gyt.at[2 * xs(i) + other], gx.at[block], x_send.at[n], x_recv.at[n], at(xs(i), z, y, other))
                )
    gx[block] = gyt[block]
    for i in range(4):
        there = feats.at[2 * xs(-i) + 1 - k]
        landed(there, f_recv.at[4 + i])
    for i in range(4):
        for kk in (0, 1):
            if i or kk:
                n = 2 * i + kk - 1
                landed(gx.at[2 * xs(-i) + lax.rem(k + kk, 2)], x_recv.at[n])
    left = jnp.concatenate([gx[b] for b in range(8)], axis=1)
    head = jnp.dot(left, feats[...].reshape(8 * B, F), preferred_element_type=jnp.float32)
    for i in range(9):
        for j in range(5):
            tile = head[16 * i : 16 * i + 16, 128 * j : 128 * j + 128]
            htf[5 * i + j] = tile
            ht[5 * i + j] = tile.astype(jnp.bfloat16)
    for n in range(TILES, PAD):
        htf[n] = jnp.zeros((16, 128), jnp.float32)
        ht[n] = jnp.zeros((16, 128), jnp.bfloat16)

    y_copies = []
    for i in (1, 2, 3):
        y_copies.append(
            start(ht.at[pl.ds(OWN * ys(i), OWN)], ry.at[i - 1], y_send.at[i - 1], y_recv.at[i - 1], at(x, z, ys(i), k))
        )
    for i in (1, 2, 3):
        landed(ry.at[i - 1], y_recv.at[i - 1])
    mine = htf[pl.ds(OWN * y, OWN)]
    for i in (0, 1, 2):
        mine = mine + ry[i].astype(jnp.float32)
    sf[...] = mine
    sb[...] = mine.astype(jnp.bfloat16)

    def z_copy(i):
        return remote(sb.at[zs(i)], rz.at[i - 1], z_send.at[i - 1], z_recv.at[i - 1], at(x, zs(i), y, k))

    for i in range(1, 16):
        @pl.when(zs(i) < OWN)
        def _():
            z_copy(i).start()

    for j in (1, 2, 3):
        landed(images.at[2 * j], i_recv.at[2 * j])
        i_copies.append(odd_image(j))
        landed(images.at[2 * j - 1], i_recv.at[2 * j - 1])
        text_side(j - 1)

    @pl.when(z < OWN)
    def _():
        for i in range(1, 16):
            landed(rz.at[i - 1], z_recv.at[i - 1])
        tile = sf[z]
        for i in range(15):
            tile = tile + rz[i].astype(jnp.float32)
        total[block, OWN * y + z] = (tile / N).astype(jnp.bfloat16)

    def a_copy(i):
        there = total.at[block, OWN * y + z]
        return remote(there, there, a_send.at[i - 1], a_recv.at[i - 1], at(x, zs(i), y, k))

    @pl.when(z < OWN)
    def _():
        for i in range(1, 16):
            a_copy(i).start()

    landed(images.at[7], i_recv.at[7])
    text_side(3)
    gt_ref[...] = back_norm(text[...].astype(jnp.float32), t_sq, grad[...]).astype(jnp.bfloat16)

    for i in range(1, 16):
        @pl.when(zs(-i) < OWN)
        def _():
            landed(total.at[block, OWN * y + zs(-i)], a_recv.at[i - 1])

    b_copies = []
    for i in (1, 2, 3):
        there = total.at[block, pl.ds(OWN * y, OWN)]
        b_copies.append(start(there, there, b_send.at[i - 1], b_recv.at[i - 1], at(x, z, ys(i), k)))
    for i in (1, 2, 3):
        landed(total.at[block, pl.ds(OWN * ys(-i), OWN)], b_recv.at[i - 1])

    c_copies = []
    there = total.at[block]
    for i in (1, 2, 3):
        c_copies.append(start(there, there, c_send.at[i], c_recv.at[i], at(xs(i), z, y, k)))
    c_copies.append(start(there, there, c_send.at[4], c_recv.at[4], sib))
    for i in (1, 2, 3):
        there = total.at[2 * xs(-i) + k]
        landed(there, c_recv.at[i])
        c_copies.append(start(there, there, c_send.at[4 + i], c_recv.at[4 + i], sib))
    for i in range(4):
        landed(total.at[2 * xs(-i) + 1 - k], c_recv.at[4 + i])
    for b in range(8):
        for i in range(9):
            for j in range(5):
                head_ref[ROWS * b + 16 * i : ROWS * b + 16 * i + 16, 128 * j : 128 * j + 128] = total[b, 5 * i + j]

    for copy in f_copies + i_copies + x_copies + y_copies + b_copies + c_copies:
        copy.wait_send()
    for i in range(1, 16):
        @pl.when(zs(i) < OWN)
        def _():
            z_copy(i).wait_send()

    @pl.when(z < OWN)
    def _():
        for i in range(1, 16):
            a_copy(i).wait_send()


def on_device(image_feats, proj_head, rest_part, text_embed, logit_scale, logit_bias):
    any_spec = pl.BlockSpec(memory_space=pl.ANY)
    vmem = pl.BlockSpec(memory_space=pltpu.VMEM)
    smem = pl.BlockSpec(memory_space=pltpu.SMEM)
    bf16, f32 = jnp.bfloat16, jnp.float32
    sems = lambda n: pltpu.SemaphoreType.DMA((n,))
    grad_text, head = pl.pallas_call(
        kernel,
        out_shape=(jax.ShapeDtypeStruct((B, D), bf16), jax.ShapeDtypeStruct((D, F), bf16)),
        in_specs=[any_spec] * 4 + [smem] * 2,
        out_specs=(vmem, vmem),
        scratch_shapes=[
            pltpu.VMEM((8, B, D), bf16),
            pltpu.VMEM((8, B, D), bf16),
            pltpu.VMEM((8, B, F), bf16),
            pltpu.VMEM((F, D), bf16),
            pltpu.VMEM((B, D), bf16),
            pltpu.VMEM((B, D), bf16),
            pltpu.VMEM((B, D), f32),
            pltpu.VMEM((B, D), f32),
            pltpu.VMEM((8, ROWS, B), bf16),
            pltpu.VMEM((8, ROWS, B), bf16),
            pltpu.VMEM((PAD, 16, 128), f32),
            pltpu.VMEM((PAD, 16, 128), bf16),
            pltpu.VMEM((3, OWN, 16, 128), bf16),
            pltpu.VMEM((OWN, 16, 128), f32),
            pltpu.VMEM((OWN, 16, 128), bf16),
            pltpu.VMEM((15, 16, 128), bf16),
            pltpu.VMEM((8, PAD, 16, 128), bf16),
            sems(4), sems(8), sems(8), sems(8), sems(8), sems(8), sems(8), sems(7), sems(7), sems(3), sems(3),
            sems(15), sems(15), sems(15), sems(15), sems(3), sems(3), sems(8), sems(8),
        ],
        compiler_params=pltpu.CompilerParams(
            collective_id=0, has_side_effects=True, vmem_limit_bytes=48 * 2**20
        ),
    )(image_feats, proj_head, rest_part, text_embed, logit_scale, logit_bias)
    return grad_text, head.T


def solution(mesh):
    placed = (P("dp", None), P(), P("dp", None), P("dp", None), P(), P())
    return jax.shard_map(
        on_device, mesh=mesh, in_specs=placed, out_specs=(P("dp", None), P()), check_vma=False
    )
```

```python
import jax
import jax.numpy as jnp
from jax import lax
from jax.experimental import pallas as pl
from jax.experimental.pallas import tpu as pltpu
from jax.sharding import PartitionSpec as P

D = 1152
F = 640
B = 128
N = 512
MESH = pl.DeviceIdType.MESH
ROWS = 144
TILES = 45
OWN = 12
PARTS = 3
HALF = B // 2


def unit_rows(values):
    squares = jnp.sum(values * values, axis=-1, keepdims=True) + 1e-06
    return squares, (values / jnp.sqrt(squares)).astype(jnp.bfloat16)


def back_norm(values, squares, grads):
    inner = jnp.sum(values * grads, axis=-1, keepdims=True)
    return (grads - values * (inner / squares)) / jnp.sqrt(squares)


def coefficients(left, right, scale, bias, first):
    logits = bias + scale * lax.dot_general(
        left, right, (((1,), (1,)), ((), ())), preferred_element_type=jnp.float32
    )
    coef = scale * jax.nn.sigmoid(logits)
    if first:
        row = lax.broadcasted_iota(jnp.int32, logits.shape, 0)
        col = lax.broadcasted_iota(jnp.int32, logits.shape, 1)
        coef = jnp.where(row == col, -scale * jax.nn.sigmoid(-logits), coef)
    return coef.astype(jnp.bfloat16)


def kernel(
    feats_hbm, proj_hbm, rest_hbm, text_hbm, scale_ref, bias_ref,
    gt_ref, head_ref,
    texts, images, feats, proj, rest, text, yv, grad, gyt, gx, htf, ht, ry, sf, sb, rz, total, headt,
    reach, load, t_send, t_recv, i_send, i_recv, f_send, f_recv, x_send, x_recv, y_send, y_recv,
    z_send, z_recv, a_send, a_recv, b_send, b_recv, c_send, c_recv,
):
    me = lax.axis_index("dp")
    k = lax.rem(me, 2)
    y = lax.rem(lax.div(me, 2), 4)
    z = lax.rem(lax.div(me, 8), 16)
    x = lax.div(me, 128)
    sib = me + 1 - 2 * k
    block = 2 * x + k

    def ring(delta):
        return lax.rem(me + (delta + N), N)

    def at(ax, az, ay, ak):
        return ((ax * 16 + az) * 4 + ay) * 2 + ak

    def xs(i):
        return lax.rem(x + (i + 4), 4)

    def ys(i):
        return lax.rem(y + (i + 4), 4)

    def zs(i):
        return lax.rem(z + (i + 16), 16)

    def remote(src, dst, send, recv, device):
        return pltpu.make_async_remote_copy(
            src_ref=src, dst_ref=dst, send_sem=send, recv_sem=recv,
            device_id=(device,), device_id_type=MESH,
        )

    def start(*args):
        copy = remote(*args)
        copy.start()
        return copy

    def landed(dst, recv):
        remote(dst, dst, t_send.at[0], recv, sib).wait_recv()

    loads = [
        pltpu.make_async_copy(text_hbm, text, load.at[0]),
        pltpu.make_async_copy(feats_hbm, feats.at[block], load.at[1]),
        pltpu.make_async_copy(proj_hbm, proj, load.at[2]),
        pltpu.make_async_copy(rest_hbm, rest, load.at[3]),
    ]
    for copy in loads:
        copy.start()

    plane = [(2, 2), (2, 1), (2, 3), (1, 2), (3, 2), (1, 1), (1, 3), (3, 1), (3, 3), (0, 2), (2, 0), (1, 0), (3, 0), (0, 1), (0, 3)]
    barrier = pltpu.get_barrier_semaphore()
    partners = [ring(d) for d in (2, -2, 6, -6, 8, -8)] + [sib, ring(-7 + 14 * k)]
    partners += [at(xs(i), z, y, 1 - k) for i in (1, 2, 3)]
    partners += [at(xs(i), z, ys(j), k) for i, j in plane]
    partners += [at(x, zs(i), y, k) for i in (1, -1)]
    for device in partners:
        pl.semaphore_signal(barrier, inc=1, device_id=(device,), device_id_type=MESH)

    def tell(n, distance):
        for i in (distance, -distance):
            pl.semaphore_signal(reach.at[n], inc=1, device_id=(at(x, zs(i), y, k),), device_id_type=MESH)

    scale = scale_ref[0]
    bias = bias_ref[0]

    loads[0].wait()
    t_sq, t_unit = unit_rows(text[...].astype(jnp.float32))
    texts[0] = t_unit
    pl.semaphore_wait(barrier, len(partners))
    tell(0, 1)

    low, high = pl.ds(0, HALF), pl.ds(HALF, HALF)
    halves = (low, high)
    at_end = lax.div(y, 3)
    at_start = lax.div(3 - y, 3)
    inner = at_end + at_start == 0
    t_copies = []
    for h, rows in enumerate(halves):
        slot = 2 + 6 * at_end
        t_copies.append(start(texts.at[0, rows], texts.at[slot, rows], t_send.at[h], t_recv.at[slot, h], ring(2 - 8 * at_end)))
        t_copies.append(start(texts.at[0, rows], texts.at[6, rows], t_send.at[2 + h], t_recv.at[6, h], ring(6)))

    def odd_text(j):
        slot = lax.rem(2 * j + 9 - 2 * k, 8)
        device = ring(1 + 6 * k) if j == 0 else sib
        return start(texts.at[2 * j], texts.at[slot], t_send.at[4 + j], t_recv.at[slot, 0], device)

    t_copies.append(odd_text(0))

    def t_edge(h):
        return remote(texts.at[8, halves[h]], texts.at[2, halves[h]], t_send.at[8 + h], t_recv.at[2, h], ring(8))

    def t_inner(h, slot, n, delta):
        rows = halves[h]
        return remote(texts.at[slot, rows], texts.at[4, rows], t_send.at[n + h], t_recv.at[4, h], ring(delta))

    loads[1].wait()
    loads[2].wait()
    loads[3].wait()
    y_full = jnp.dot(feats[block], proj[...], preferred_element_type=jnp.float32)
    y_full = y_full + rest[...].astype(jnp.float32)
    yv[...] = y_full
    y_sq, image_unit = unit_rows(y_full)
    images[0] = image_unit
    pl.semaphore_wait(reach.at[0], 2)
    tell(1, 2)

    def pair_of(held, a, b):
        return jnp.concatenate([held[a], held[b]], axis=0)

    def gather_grad(unit, pair, first):
        coef = coefficients(unit, pair, scale, bias, first)
        part = jnp.dot(coef, pair, preferred_element_type=jnp.float32)
        if first:
            grad[...] = part
        else:
            grad[...] += part

    for h, rows in enumerate(halves):
        @pl.when(y == 0)
        def _():
            landed(texts.at[8, rows], t_recv.at[8, h])
            t_edge(h).start()

        landed(texts.at[6, rows], t_recv.at[6, h])

        @pl.when(y > 0)
        def _():
            landed(texts.at[2, rows], t_recv.at[2, h])

        @pl.when(inner)
        def _():
            t_inner(h, 6, 10, -2).start()
            t_inner(h, 2, 12, 2).start()

    t_copies.append(odd_text(3))
    pl.semaphore_wait(reach.at[1], 2)
    tell(2, 4)

    f_copies = []
    for i in (2, 1, 3):
        f_copies.append(start(feats.at[block], feats.at[block], f_send.at[i], f_recv.at[i], at(xs(i), z, y, k)))
    f_copies.append(start(feats.at[block], feats.at[block], f_send.at[4], f_recv.at[4], sib))

    landed(texts.at[1], t_recv.at[1, 0])
    gather_grad(images[0], pair_of(texts, 0, 1), True)
    landed(texts.at[7], t_recv.at[7, 0])
    gather_grad(images[0], pair_of(texts, 6, 7), False)

    @pl.when(y == 0)
    def _():
        for h, rows in enumerate(halves):
            landed(texts.at[2, rows], t_recv.at[2, h])

    t_copies.append(odd_text(1))
    landed(texts.at[5 - 2 * k], t_recv.at[5 - 2 * k, 0])
    gather_grad(images[0], pair_of(texts, 2, 5 - 2 * k), False)
    for h, rows in enumerate(halves):
        landed(texts.at[4, rows], t_recv.at[4, h])
    t_copies.append(odd_text(2))
    landed(texts.at[3 + 2 * k], t_recv.at[3 + 2 * k, 0])
    gather_grad(images[0], pair_of(texts, 4, 3 + 2 * k), False)

    grad_y = back_norm(yv[...], y_sq, grad[...]).astype(jnp.bfloat16)
    gyt[...] = jnp.transpose(grad_y.astype(jnp.float32)).astype(jnp.bfloat16).reshape(8, ROWS, B)

    x_copies = []
    across = [(2, 0), (2, 1), (1, 0), (1, 1), (3, 0), (3, 1), (0, 1)]
    for n, (i, kk) in enumerate(across):
        other = lax.rem(k + kk, 2)
        x_copies.append(
            start(gyt.at[2 * xs(i) + other], gx.at[block], x_send.at[n], x_recv.at[n], at(xs(i), z, y, other))
        )
    gx[block] = gyt[block]
    for i in (1, 3, 2):
        there = feats.at[2 * xs(-i) + k]
        landed(there, f_recv.at[i])
        f_copies.append(start(there, there, f_send.at[4 + i], f_recv.at[4 + i], sib))
    for i in range(4):
        landed(feats.at[2 * xs(-i) + 1 - k], f_recv.at[4 + i])
    for n, (i, kk) in enumerate(across):
        landed(gx.at[2 * xs(-i) + lax.rem(k + kk, 2)], x_recv.at[n])
    left = jnp.concatenate([gx[b] for b in range(8)], axis=1)
    head = jnp.dot(left, feats[...].reshape(8 * B, F), preferred_element_type=jnp.float32)
    for n in range(PARTS * 16):
        i, j = n // 5, n % 5
        if n < TILES:
            tile = head[16 * i : 16 * i + 16, 128 * j : 128 * j + 128]
        else:
            tile = jnp.zeros((16, 128), jnp.float32)
        htf[n // 16, n % 16] = tile
        ht[n // 16, n % 16] = tile.astype(jnp.bfloat16)

    y_copies = []
    for i in (2, 1, 3):
        y_copies.append(
            start(ht.at[:, pl.ds(4 * ys(i), 4)], ry.at[i - 1], y_send.at[i - 1], y_recv.at[i - 1], at(x, z, ys(i), k))
        )
    for i in (1, 3, 2):
        landed(ry.at[i - 1], y_recv.at[i - 1])
    mine = htf[:, pl.ds(4 * y, 4)]
    for i in (0, 1, 2):
        mine = mine + ry[i].astype(jnp.float32)
    mine = mine.reshape(OWN, 16, 128)
    sf[...] = mine
    sb[...] = mine.astype(jnp.bfloat16)

    far_first = (8, 7, 9, 6, 10, 5, 11, 4, 12, 3, 13, 2, 14, 1, 15)
    w = lax.rem(z + 12, 16)

    def ws(i):
        return lax.rem(w + (i + 16), 16)

    def z_copy(i):
        return remote(sb.at[ws(i)], rz.at[i - 1], z_send.at[i - 1], z_recv.at[i - 1], at(x, zs(i), y, k))

    pl.semaphore_wait(reach.at[2], 2)
    for i in far_first:
        @pl.when(ws(i) < OWN)
        def _():
            z_copy(i).start()

    i_copies = []
    for h, rows in enumerate(halves):
        slot = 2 + 6 * at_start
        i_copies.append(start(images.at[0, rows], images.at[slot, rows], i_send.at[h], i_recv.at[slot, h], ring(8 * at_start - 2)))
        i_copies.append(start(images.at[0, rows], images.at[6, rows], i_send.at[2 + h], i_recv.at[6, h], ring(-6)))

    def odd_image(j):
        slot = lax.rem(2 * j + 7 + 2 * k, 8)
        device = ring(-7 + 6 * k) if j == 0 else sib
        return start(images.at[2 * j], images.at[slot], i_send.at[4 + j], i_recv.at[slot, 0], device)

    i_copies.append(odd_image(0))

    def i_edge(h):
        return remote(images.at[8, halves[h]], images.at[2, halves[h]], i_send.at[8 + h], i_recv.at[2, h], ring(-8))

    def i_inner(h, slot, n, delta):
        rows = halves[h]
        return remote(images.at[slot, rows], images.at[4, rows], i_send.at[n + h], i_recv.at[4, h], ring(delta))

    def pass_on_images(h):
        rows = halves[h]

        @pl.when(y == 3)
        def _():
            landed(images.at[8, rows], i_recv.at[8, h])
            i_edge(h).start()

        landed(images.at[6, rows], i_recv.at[6, h])

        @pl.when(y < 3)
        def _():
            landed(images.at[2, rows], i_recv.at[2, h])

        @pl.when(inner)
        def _():
            i_inner(h, 6, 10, 2).start()
            i_inner(h, 2, 12, -2).start()

    pass_on_images(0)

    part = lax.div(w, 4)
    own = total.at[block, part, 4 * y + lax.rem(w, 4)]

    @pl.when(w < OWN)
    def _():
        for i in range(1, 16):
            landed(rz.at[i - 1], z_recv.at[i - 1])
        tile = sf[w]
        for i in range(15):
            tile = tile + rz[i].astype(jnp.float32)
        own[...] = (tile / N).astype(jnp.bfloat16)

    def a_copy(i):
        return remote(own, own, a_send.at[i - 1], a_recv.at[w], at(x, zs(i), y, k))

    @pl.when(w < OWN)
    def _():
        for i in far_first:
            a_copy(i).start()

    pass_on_images(1)
    i_copies.append(odd_image(3))
    landed(images.at[1], i_recv.at[1, 0])
    gather_grad(texts[0], pair_of(images, 0, 1), True)
    landed(images.at[7], i_recv.at[7, 0])
    gather_grad(texts[0], pair_of(images, 6, 7), False)

    first = part - lax.div(w, 12)
    last = lax.rem(lax.div(w, 6) + 2, 3)
    b_copies = []
    parts = (first, 3 - first - last, last)
    for n, q in enumerate(parts):
        for r in range(4):
            owner = 4 * q + r

            @pl.when(owner != w)
            def _():
                landed(total.at[block, q, 4 * y + r], a_recv.at[owner])

        there = total.at[block, q, pl.ds(4 * y, 4)]
        for m, (i, j) in enumerate(plane):
            b_copies.append(start(there, there, b_send.at[n, m], b_recv.at[n, m], at(xs(i), z, ys(j), k)))

    @pl.when(y == 3)
    def _():
        for h, rows in enumerate(halves):
            landed(images.at[2, rows], i_recv.at[2, h])

    i_copies.append(odd_image(1))
    for h, rows in enumerate(halves):
        landed(images.at[4, rows], i_recv.at[4, h])
    i_copies.append(odd_image(2))
    landed(images.at[3 + 2 * k], i_recv.at[3 + 2 * k, 0])
    gather_grad(texts[0], pair_of(images, 2, 3 + 2 * k), False)
    landed(images.at[5 - 2 * k], i_recv.at[5 - 2 * k, 0])
    gather_grad(texts[0], pair_of(images, 4, 5 - 2 * k), False)
    gt_ref[...] = back_norm(text[...].astype(jnp.float32), t_sq, grad[...]).astype(jnp.bfloat16)

    c_copies = []
    for n, q in enumerate(parts):
        for i in range(4):
            for m, (pi, pj) in enumerate(plane):
                if pi == i:
                    landed(total.at[2 * xs(-pi) + k, q, pl.ds(4 * ys(-pj), 4)], b_recv.at[n, m])
            there = total.at[2 * xs(-i) + k, q]
            c_copies.append(start(there, there, c_send.at[n, i], c_recv.at[n, i], sib))
    for n, q in enumerate(parts):
        for i in range(4):
            landed(total.at[2 * xs(-i) + 1 - k, q], c_recv.at[n, i])
    for b in range(8):
        for n in range(TILES):
            i, j = n // 5, n % 5
            headt[ROWS * b + 16 * i : ROWS * b + 16 * i + 16, 128 * j : 128 * j + 128] = total[b, n // 16, n % 16]

    for i in range(9):
        for j in range(5):
            block_t = headt[128 * i : 128 * i + 128, 128 * j : 128 * j + 128].astype(jnp.float32)
            head_ref[128 * j : 128 * j + 128, 128 * i : 128 * i + 128] = jnp.transpose(block_t).astype(jnp.bfloat16)

    for copy in t_copies + f_copies + i_copies + x_copies + y_copies + b_copies + c_copies:
        copy.wait_send()
    for i in far_first:
        @pl.when(ws(i) < OWN)
        def _():
            z_copy(i).wait_send()

    @pl.when(y == 0)
    def _():
        for h in (0, 1):
            t_edge(h).wait_send()

    @pl.when(y == 3)
    def _():
        for h in (0, 1):
            i_edge(h).wait_send()

    @pl.when(inner)
    def _():
        for h in (0, 1):
            t_inner(h, 6, 10, -2).wait_send()
            t_inner(h, 2, 12, 2).wait_send()
            i_inner(h, 6, 10, 2).wait_send()
            i_inner(h, 2, 12, -2).wait_send()

    @pl.when(w < OWN)
    def _():
        for i in far_first:
            a_copy(i).wait_send()


def on_device(image_feats, proj_head, rest_part, text_embed, logit_scale, logit_bias):
    any_spec = pl.BlockSpec(memory_space=pl.ANY)
    vmem = pl.BlockSpec(memory_space=pltpu.VMEM)
    smem = pl.BlockSpec(memory_space=pltpu.SMEM)
    bf16, f32 = jnp.bfloat16, jnp.float32
    sems = lambda *n: pltpu.SemaphoreType.DMA(n)
    grad_text, head = pl.pallas_call(
        kernel,
        out_shape=(jax.ShapeDtypeStruct((B, D), bf16), jax.ShapeDtypeStruct((F, D), bf16)),
        in_specs=[any_spec] * 4 + [smem] * 2,
        out_specs=(vmem, vmem),
        scratch_shapes=[
            pltpu.VMEM((9, B, D), bf16),
            pltpu.VMEM((9, B, D), bf16),
            pltpu.VMEM((8, B, F), bf16),
            pltpu.VMEM((F, D), bf16),
            pltpu.VMEM((B, D), bf16),
            pltpu.VMEM((B, D), bf16),
            pltpu.VMEM((B, D), f32),
            pltpu.VMEM((B, D), f32),
            pltpu.VMEM((8, ROWS, B), bf16),
            pltpu.VMEM((8, ROWS, B), bf16),
            pltpu.VMEM((PARTS, 16, 16, 128), f32),
            pltpu.VMEM((PARTS, 16, 16, 128), bf16),
            pltpu.VMEM((3, PARTS, 4, 16, 128), bf16),
            pltpu.VMEM((OWN, 16, 128), f32),
            pltpu.VMEM((OWN, 16, 128), bf16),
            pltpu.VMEM((15, 16, 128), bf16),
            pltpu.VMEM((8, PARTS, 16, 16, 128), bf16),
            pltpu.VMEM((D, F), bf16),
            pltpu.SemaphoreType.REGULAR((3,)), sems(4), sems(14), sems(9, 2), sems(14), sems(9, 2), sems(8), sems(8), sems(7), sems(7), sems(3), sems(3),
            sems(15), sems(15), sems(15), sems(12), sems(3, 15), sems(3, 15), sems(3, 4), sems(3, 4),
        ],
        compiler_params=pltpu.CompilerParams(
            collective_id=0, has_side_effects=True, vmem_limit_bytes=60 * 2**20
        ),
    )(image_feats, proj_head, rest_part, text_embed, logit_scale, logit_bias)
    return grad_text, head


def solution(mesh):
    placed = (P("dp", None), P(), P("dp", None), P("dp", None), P(), P())
    return jax.shard_map(
        on_device, mesh=mesh, in_specs=placed, out_specs=(P("dp", None), P()), check_vma=False
    )
```

```python
import jax
import jax.numpy as jnp
from jax import lax
from jax.experimental import pallas as pl
from jax.experimental.pallas import tpu as pltpu
from jax.sharding import PartitionSpec as P

D = 1152
F = 640
B = 128
N = 512
MESH = pl.DeviceIdType.MESH
ROWS = 144
TILES = 45
OWN = 12
PARTS = 3
HALF = B // 2


def unit_rows(values):
    squares = jnp.sum(values * values, axis=-1, keepdims=True) + 1e-06
    return squares, (values / jnp.sqrt(squares)).astype(jnp.bfloat16)


def back_norm(values, squares, grads):
    inner = jnp.sum(values * grads, axis=-1, keepdims=True)
    return (grads - values * (inner / squares)) / jnp.sqrt(squares)


def coefficients(left, right, scale, bias, first):
    logits = bias + scale * lax.dot_general(
        left, right, (((1,), (1,)), ((), ())), preferred_element_type=jnp.float32
    )
    coef = scale * jax.nn.sigmoid(logits)
    if first:
        row = lax.broadcasted_iota(jnp.int32, logits.shape, 0)
        col = lax.broadcasted_iota(jnp.int32, logits.shape, 1)
        coef = jnp.where(row == col, -scale * jax.nn.sigmoid(-logits), coef)
    return coef.astype(jnp.bfloat16)


def kernel(
    feats_hbm, proj_hbm, rest_hbm, text_hbm, scale_ref, bias_ref,
    gt_ref, head_ref,
    texts, images, feats, proj, rest, text, yv, grad, gyt, gx, htf, ht, ry, sf, sb, rz, total, headt,
    reach, load, t_send, t_recv, i_send, i_recv, f_send, f_recv, x_send, x_recv, y_send, y_recv,
    z_send, z_recv, a_send, a_recv, b_send, b_recv, c_send, c_recv,
):
    me = lax.axis_index("dp")
    k = lax.rem(me, 2)
    y = lax.rem(lax.div(me, 2), 4)
    z = lax.rem(lax.div(me, 8), 16)
    x = lax.div(me, 128)
    sib = me + 1 - 2 * k
    block = 2 * x + k

    def ring(delta):
        return lax.rem(me + (delta + N), N)

    def at(ax, az, ay, ak):
        return ((ax * 16 + az) * 4 + ay) * 2 + ak

    def xs(i):
        return lax.rem(x + (i + 4), 4)

    def ys(i):
        return lax.rem(y + (i + 4), 4)

    def zs(i):
        return lax.rem(z + (i + 16), 16)

    def remote(src, dst, send, recv, device):
        return pltpu.make_async_remote_copy(
            src_ref=src, dst_ref=dst, send_sem=send, recv_sem=recv,
            device_id=(device,), device_id_type=MESH,
        )

    def start(*args):
        copy = remote(*args)
        copy.start()
        return copy

    def landed(dst, recv):
        remote(dst, dst, t_send.at[0], recv, sib).wait_recv()

    loads = [
        pltpu.make_async_copy(text_hbm, text, load.at[0]),
        pltpu.make_async_copy(feats_hbm, feats.at[block], load.at[1]),
        pltpu.make_async_copy(proj_hbm, proj, load.at[2]),
        pltpu.make_async_copy(rest_hbm, rest, load.at[3]),
    ]
    for copy in loads:
        copy.start()

    plane = [(2, 2), (2, 1), (2, 3), (1, 2), (3, 2), (1, 1), (1, 3), (3, 1), (3, 3), (0, 2), (2, 0), (1, 0), (3, 0), (0, 1), (0, 3)]
    barrier = pltpu.get_barrier_semaphore()
    partners = [ring(d) for d in (2, -2, 6, -6, 8, -8)] + [sib, ring(-7 + 14 * k)]
    partners += [at(xs(i), z, y, 1 - k) for i in (1, 2, 3)]
    partners += [at(xs(i), z, ys(j), k) for i, j in plane if i == 0 or j == 0]
    partners += [at(x, zs(i), y, k) for i in (1, -1)]
    for device in partners:
        pl.semaphore_signal(barrier, inc=1, device_id=(device,), device_id_type=MESH)

    def tell(n, distance):
        for i in (distance, -distance):
            pl.semaphore_signal(reach.at[n], inc=1, device_id=(at(x, zs(i), y, k),), device_id_type=MESH)

    scale = scale_ref[0]
    bias = bias_ref[0]

    loads[0].wait()
    t_sq, t_unit = unit_rows(text[...].astype(jnp.float32))
    texts[0] = t_unit
    pl.semaphore_wait(barrier, len(partners))
    tell(0, 1)

    low, high = pl.ds(0, HALF), pl.ds(HALF, HALF)
    halves = (low, high)
    at_end = lax.div(y, 3)
    at_start = lax.div(3 - y, 3)
    inner = at_end + at_start == 0
    t_copies = []
    for h, rows in enumerate(halves):
        slot = 2 + 6 * at_end
        t_copies.append(start(texts.at[0, rows], texts.at[slot, rows], t_send.at[h], t_recv.at[slot, h], ring(2 - 8 * at_end)))
        t_copies.append(start(texts.at[0, rows], texts.at[6, rows], t_send.at[2 + h], t_recv.at[6, h], ring(6)))

    def odd_text(j):
        slot = lax.rem(2 * j + 9 - 2 * k, 8)
        device = ring(1 + 6 * k) if j == 0 else sib
        return start(texts.at[2 * j], texts.at[slot], t_send.at[4 + j], t_recv.at[slot, 0], device)

    t_copies.append(odd_text(0))

    def t_edge(h):
        return remote(texts.at[8, halves[h]], texts.at[2, halves[h]], t_send.at[8 + h], t_recv.at[2, h], ring(8))

    def t_inner(h, slot, n, delta):
        rows = halves[h]
        return remote(texts.at[slot, rows], texts.at[4, rows], t_send.at[n + h], t_recv.at[4, h], ring(delta))

    loads[1].wait()
    loads[2].wait()
    loads[3].wait()
    y_full = jnp.dot(feats[block], proj[...], preferred_element_type=jnp.float32)
    y_full = y_full + rest[...].astype(jnp.float32)
    yv[...] = y_full
    y_sq, image_unit = unit_rows(y_full)
    images[0] = image_unit
    pl.semaphore_wait(reach.at[0], 2)
    tell(1, 2)

    def pair_of(held, a, b):
        return jnp.concatenate([held[a], held[b]], axis=0)

    def gather_grad(unit, pair, first):
        coef = coefficients(unit, pair, scale, bias, first)
        part = jnp.dot(coef, pair, preferred_element_type=jnp.float32)
        if first:
            grad[...] = part
        else:
            grad[...] += part

    for h, rows in enumerate(halves):
        @pl.when(y == 0)
        def _():
            landed(texts.at[8, rows], t_recv.at[8, h])
            t_edge(h).start()

        landed(texts.at[6, rows], t_recv.at[6, h])

        @pl.when(y > 0)
        def _():
            landed(texts.at[2, rows], t_recv.at[2, h])

        @pl.when(inner)
        def _():
            t_inner(h, 6, 10, -2).start()
            t_inner(h, 2, 12, 2).start()

    t_copies.append(odd_text(3))
    pl.semaphore_wait(reach.at[1], 2)
    tell(2, 4)

    def image_copy(n):
        if n == 0:
            slot = 2 + 6 * at_start
            return remote(images.at[0], images.at[slot], i_send.at[0], i_recv.at[slot], ring(8 * at_start - 2))
        return remote(images.at[0], images.at[6], i_send.at[1], i_recv.at[6], ring(-6))

    def odd_image(j):
        slot = lax.rem(2 * j + 7 + 2 * k, 8)
        device = ring(-7 + 6 * k) if j == 0 else sib
        return start(images.at[2 * j], images.at[slot], i_send.at[4 + j], i_recv.at[slot], device)

    image_edge = remote(images.at[8], images.at[2], i_send.at[2], i_recv.at[2], ring(-8))
    image_inner = [
        remote(images.at[6], images.at[4], i_send.at[3], i_recv.at[4], ring(2)),
        remote(images.at[2], images.at[4], i_send.at[8], i_recv.at[4], ring(-2)),
    ]

    @pl.when(jnp.logical_not(inner))
    def _():
        image_copy(0).start()
        image_copy(1).start()

    f_copies = []
    for i in (2, 1, 3):
        f_copies.append(start(feats.at[block], feats.at[block], f_send.at[i], f_recv.at[i], at(xs(i), z, y, k)))
    f_copies.append(start(feats.at[block], feats.at[block], f_send.at[4], f_recv.at[4], sib))

    landed(texts.at[1], t_recv.at[1, 0])
    gather_grad(images[0], pair_of(texts, 0, 1), True)
    landed(texts.at[7], t_recv.at[7, 0])
    gather_grad(images[0], pair_of(texts, 6, 7), False)

    @pl.when(y == 0)
    def _():
        for h, rows in enumerate(halves):
            landed(texts.at[2, rows], t_recv.at[2, h])

    t_copies.append(odd_text(1))
    landed(texts.at[5 - 2 * k], t_recv.at[5 - 2 * k, 0])
    gather_grad(images[0], pair_of(texts, 2, 5 - 2 * k), False)
    for h, rows in enumerate(halves):
        landed(texts.at[4, rows], t_recv.at[4, h])
    t_copies.append(odd_text(2))
    landed(texts.at[3 + 2 * k], t_recv.at[3 + 2 * k, 0])
    gather_grad(images[0], pair_of(texts, 4, 3 + 2 * k), False)

    grad_y = back_norm(yv[...], y_sq, grad[...]).astype(jnp.bfloat16)
    gyt[...] = jnp.transpose(grad_y.astype(jnp.float32)).astype(jnp.bfloat16).reshape(8, ROWS, B)

    x_copies = []
    across = [(2, 0), (2, 1), (1, 0), (1, 1), (3, 0), (3, 1), (0, 1)]
    for n, (i, kk) in enumerate(across):
        other = lax.rem(k + kk, 2)
        x_copies.append(
            start(gyt.at[2 * xs(i) + other], gx.at[block], x_send.at[n], x_recv.at[n], at(xs(i), z, y, other))
        )
    @pl.when(inner)
    def _():
        image_copy(0).start()

    @pl.when(jnp.logical_and(inner, z > 0))
    def _():
        image_copy(1).start()

    gx[block] = gyt[block]
    for i in (1, 3, 2):
        there = feats.at[2 * xs(-i) + k]
        landed(there, f_recv.at[i])
        f_copies.append(start(there, there, f_send.at[4 + i], f_recv.at[4 + i], sib))
    for i in range(4):
        landed(feats.at[2 * xs(-i) + 1 - k], f_recv.at[4 + i])
    for n, (i, kk) in enumerate(across):
        landed(gx.at[2 * xs(-i) + lax.rem(k + kk, 2)], x_recv.at[n])
    left = jnp.concatenate([gx[b] for b in range(8)], axis=1)
    head = jnp.dot(left, feats[...].reshape(8 * B, F), preferred_element_type=jnp.float32)
    for n in range(PARTS * 16):
        i, j = n // 5, n % 5
        if n < TILES:
            tile = head[16 * i : 16 * i + 16, 128 * j : 128 * j + 128]
        else:
            tile = jnp.zeros((16, 128), jnp.float32)
        htf[n // 16, n % 16] = tile
        ht[n // 16, n % 16] = tile.astype(jnp.bfloat16)

    y_copies = []
    for i in (2, 1, 3):
        y_copies.append(
            start(ht.at[:, pl.ds(4 * ys(i), 4)], ry.at[i - 1], y_send.at[i - 1], y_recv.at[i - 1], at(x, z, ys(i), k))
        )
    @pl.when(y == 3)
    def _():
        landed(images.at[8], i_recv.at[8])
        image_edge.start()

    for i in (1, 3, 2):
        landed(ry.at[i - 1], y_recv.at[i - 1])
    mine = htf[:, pl.ds(4 * y, 4)]
    for i in (0, 1, 2):
        mine = mine + ry[i].astype(jnp.float32)
    mine = mine.reshape(OWN, 16, 128)
    sf[...] = mine
    sb[...] = mine.astype(jnp.bfloat16)

    far_first = (8, 7, 9, 6, 10, 5, 11, 4, 12, 3, 13, 2, 14, 1, 15)
    w = lax.rem(z + 12, 16)

    def ws(i):
        return lax.rem(w + (i + 16), 16)

    def z_copy(i):
        return remote(sb.at[ws(i)], rz.at[i - 1], z_send.at[i - 1], z_recv.at[i - 1], at(x, zs(i), y, k))

    pl.semaphore_wait(reach.at[2], 2)
    for i in far_first:
        @pl.when(ws(i) < OWN)
        def _():
            z_copy(i).start()

    @pl.when(jnp.logical_and(inner, z == 0))
    def _():
        image_copy(1).start()

    i_copies = [odd_image(0)]

    landed(images.at[6], i_recv.at[6])
    landed(images.at[2], i_recv.at[2])

    @pl.when(inner)
    def _():
        for copy in image_inner:
            copy.start()

    part = lax.div(w, 4)
    own = total.at[block, part, 4 * y + lax.rem(w, 4)]

    @pl.when(w < OWN)
    def _():
        for i in range(1, 16):
            landed(rz.at[i - 1], z_recv.at[i - 1])
        tile = sf[w]
        for i in range(15):
            tile = tile + rz[i].astype(jnp.float32)
        own[...] = (tile / N).astype(jnp.bfloat16)

    def a_copy(i):
        return remote(own, own, a_send.at[i - 1], a_recv.at[w], at(x, zs(i), y, k))

    @pl.when(w < OWN)
    def _():
        for i in far_first:
            a_copy(i).start()

    i_copies += [odd_image(3), odd_image(1)]
    landed(images.at[1], i_recv.at[1])
    gather_grad(texts[0], pair_of(images, 0, 1), True)
    landed(images.at[7], i_recv.at[7])
    gather_grad(texts[0], pair_of(images, 6, 7), False)
    landed(images.at[3 + 2 * k], i_recv.at[3 + 2 * k])
    gather_grad(texts[0], pair_of(images, 2, 3 + 2 * k), False)

    landed(images.at[4], i_recv.at[4])
    i_copies.append(odd_image(2))
    landed(images.at[5 - 2 * k], i_recv.at[5 - 2 * k])
    gather_grad(texts[0], pair_of(images, 4, 5 - 2 * k), False)
    gt_ref[...] = back_norm(text[...].astype(jnp.float32), t_sq, grad[...]).astype(jnp.bfloat16)

    first = part - lax.div(w, 12)
    last = lax.rem(lax.div(w, 6) + 2, 3)
    b_copies = []
    parts = (first, 3 - first - last, last)
    for n, q in enumerate(parts):
        for r in range(4):
            owner = 4 * q + r

            @pl.when(owner != w)
            def _():
                landed(total.at[block, q, 4 * y + r], a_recv.at[owner])

        there = total.at[block, q, pl.ds(4 * y, 4)]
        for m, (i, j) in enumerate(plane):
            b_copies.append(start(there, there, b_send.at[n, m], b_recv.at[n, m], at(xs(i), z, ys(j), k)))

    c_copies = []
    for n, q in enumerate(parts):
        for i in range(4):
            for m, (pi, pj) in enumerate(plane):
                if pi == i:
                    landed(total.at[2 * xs(-pi) + k, q, pl.ds(4 * ys(-pj), 4)], b_recv.at[n, m])
            there = total.at[2 * xs(-i) + k, q]
            c_copies.append(start(there, there, c_send.at[n, i], c_recv.at[n, i], sib))
    for n, q in enumerate(parts):
        for i in range(4):
            landed(total.at[2 * xs(-i) + 1 - k, q], c_recv.at[n, i])
    for b in range(8):
        for n in range(TILES):
            i, j = n // 5, n % 5
            headt[ROWS * b + 16 * i : ROWS * b + 16 * i + 16, 128 * j : 128 * j + 128] = total[b, n // 16, n % 16]

    for i in range(9):
        for j in range(5):
            block_t = headt[128 * i : 128 * i + 128, 128 * j : 128 * j + 128].astype(jnp.float32)
            head_ref[128 * j : 128 * j + 128, 128 * i : 128 * i + 128] = jnp.transpose(block_t).astype(jnp.bfloat16)

    for copy in t_copies + f_copies + i_copies + x_copies + y_copies + b_copies + c_copies:
        copy.wait_send()
    for i in far_first:
        @pl.when(ws(i) < OWN)
        def _():
            z_copy(i).wait_send()

    @pl.when(y == 0)
    def _():
        for h in (0, 1):
            t_edge(h).wait_send()

    image_copy(0).wait_send()
    image_copy(1).wait_send()

    @pl.when(y == 3)
    def _():
        image_edge.wait_send()

    @pl.when(inner)
    def _():
        for h in (0, 1):
            t_inner(h, 6, 10, -2).wait_send()
            t_inner(h, 2, 12, 2).wait_send()
        for copy in image_inner:
            copy.wait_send()

    @pl.when(w < OWN)
    def _():
        for i in far_first:
            a_copy(i).wait_send()


def on_device(image_feats, proj_head, rest_part, text_embed, logit_scale, logit_bias):
    any_spec = pl.BlockSpec(memory_space=pl.ANY)
    vmem = pl.BlockSpec(memory_space=pltpu.VMEM)
    smem = pl.BlockSpec(memory_space=pltpu.SMEM)
    bf16, f32 = jnp.bfloat16, jnp.float32
    sems = lambda *n: pltpu.SemaphoreType.DMA(n)
    grad_text, head = pl.pallas_call(
        kernel,
        out_shape=(pltpu.VMEM((B, D), bf16), pltpu.VMEM((F, D), bf16)),
        in_specs=[any_spec] * 4 + [smem] * 2,
        out_specs=(vmem, vmem),
        scratch_shapes=[
            pltpu.VMEM((9, B, D), bf16),
            pltpu.VMEM((9, B, D), bf16),
            pltpu.VMEM((8, B, F), bf16),
            pltpu.VMEM((F, D), bf16),
            pltpu.VMEM((B, D), bf16),
            pltpu.VMEM((B, D), bf16),
            pltpu.VMEM((B, D), f32),
            pltpu.VMEM((B, D), f32),
            pltpu.VMEM((8, ROWS, B), bf16),
            pltpu.VMEM((8, ROWS, B), bf16),
            pltpu.VMEM((PARTS, 16, 16, 128), f32),
            pltpu.VMEM((PARTS, 16, 16, 128), bf16),
            pltpu.VMEM((3, PARTS, 4, 16, 128), bf16),
            pltpu.VMEM((OWN, 16, 128), f32),
            pltpu.VMEM((OWN, 16, 128), bf16),
            pltpu.VMEM((15, 16, 128), bf16),
            pltpu.VMEM((8, PARTS, 16, 16, 128), bf16),
            pltpu.VMEM((D, F), bf16),
            pltpu.SemaphoreType.REGULAR((3,)), sems(4), sems(14), sems(9, 2), sems(9), sems(9), sems(8), sems(8), sems(7), sems(7), sems(3), sems(3),
            sems(15), sems(15), sems(15), sems(12), sems(3, 15), sems(3, 15), sems(3, 4), sems(3, 4),
        ],
        compiler_params=pltpu.CompilerParams(
            collective_id=0, has_side_effects=True, vmem_limit_bytes=60 * 2**20
        ),
    )(image_feats, proj_head, rest_part, text_embed, logit_scale, logit_bias)
    return grad_text, head


def solution(mesh):
    placed = (P("dp", None), P(), P("dp", None), P("dp", None), P(), P())
    return jax.shard_map(
        on_device, mesh=mesh, in_specs=placed, out_specs=(P("dp", None), P()), check_vma=False
    )
```

```python
import jax
import jax.numpy as jnp
from jax import lax
from jax.experimental import pallas as pl
from jax.experimental.pallas import tpu as pltpu
from jax.sharding import PartitionSpec as P

D = 1152
F = 640
B = 128
N = 512
MESH = pl.DeviceIdType.MESH
ROWS = 144
TILES = 45
OWN = 12
PARTS = 3
HALF = B // 2


def unit_rows(values):
    squares = jnp.sum(values * values, axis=-1, keepdims=True) + 1e-06
    return squares, (values / jnp.sqrt(squares)).astype(jnp.bfloat16)


def back_norm(values, squares, grads):
    inner = jnp.sum(values * grads, axis=-1, keepdims=True)
    return (grads - values * (inner / squares)) / jnp.sqrt(squares)


def coefficients(left, right, scale, bias, first):
    logits = bias + scale * lax.dot_general(
        left, right, (((1,), (1,)), ((), ())), preferred_element_type=jnp.float32
    )
    coef = scale * jax.nn.sigmoid(logits)
    if first:
        row = lax.broadcasted_iota(jnp.int32, logits.shape, 0)
        col = lax.broadcasted_iota(jnp.int32, logits.shape, 1)
        coef = jnp.where(row == col, -scale * jax.nn.sigmoid(-logits), coef)
    return coef.astype(jnp.bfloat16)


def kernel(
    feats_hbm, proj_hbm, rest_hbm, text_hbm, scale_ref, bias_ref,
    gt_ref, head_ref,
    texts, images, feats, proj, rest, text, yv, grad, gyt, gx, htf, ht, ry, sf, sb, rz, total, headt,
    reach, load, t_send, t_recv, i_send, i_recv, f_send, f_recv, x_send, x_recv, y_send, y_recv,
    z_send, z_recv, a_send, a_recv, b_send, b_recv, c_send, c_recv,
):
    me = lax.axis_index("dp")
    k = lax.rem(me, 2)
    y = lax.rem(lax.div(me, 2), 4)
    z = lax.rem(lax.div(me, 8), 16)
    x = lax.div(me, 128)
    sib = me + 1 - 2 * k
    block = 2 * x + k

    def ring(delta):
        return lax.rem(me + (delta + N), N)

    def at(ax, az, ay, ak):
        return ((ax * 16 + az) * 4 + ay) * 2 + ak

    def xs(i):
        return lax.rem(x + (i + 4), 4)

    def ys(i):
        return lax.rem(y + (i + 4), 4)

    def zs(i):
        return lax.rem(z + (i + 16), 16)

    def remote(src, dst, send, recv, device):
        return pltpu.make_async_remote_copy(
            src_ref=src, dst_ref=dst, send_sem=send, recv_sem=recv,
            device_id=(device,), device_id_type=MESH,
        )

    def start(*args):
        copy = remote(*args)
        copy.start()
        return copy

    def landed(dst, recv):
        remote(dst, dst, t_send.at[0], recv, sib).wait_recv()

    loads = [
        pltpu.make_async_copy(text_hbm, text, load.at[0]),
        pltpu.make_async_copy(feats_hbm, feats.at[block], load.at[1]),
        pltpu.make_async_copy(proj_hbm, proj, load.at[2]),
        pltpu.make_async_copy(rest_hbm, rest, load.at[3]),
    ]
    for copy in loads:
        copy.start()

    plane = [(2, 2), (2, 1), (2, 3), (1, 2), (3, 2), (1, 1), (1, 3), (3, 1), (3, 3), (0, 2), (2, 0), (1, 0), (3, 0), (0, 1), (0, 3)]
    barrier = pltpu.get_barrier_semaphore()
    partners = [ring(d) for d in (2, -2, 6, -6, 8, -8)] + [sib, ring(-7 + 14 * k)]
    partners += [at(xs(i), z, y, 1 - k) for i in (1, 2, 3)]
    partners += [at(xs(i), z, ys(j), k) for i, j in plane if i == 0 or j == 0]
    partners += [at(x, zs(i), y, k) for i in (1, -1)]
    for device in partners:
        pl.semaphore_signal(barrier, inc=1, device_id=(device,), device_id_type=MESH)

    def tell(n, distance):
        for i in (distance, -distance):
            pl.semaphore_signal(reach.at[n], inc=1, device_id=(at(x, zs(i), y, k),), device_id_type=MESH)

    scale = scale_ref[0]
    bias = bias_ref[0]

    loads[0].wait()
    t_sq, t_unit = unit_rows(text[...].astype(jnp.float32))
    texts[0] = t_unit
    pl.semaphore_wait(barrier, len(partners))
    tell(0, 1)

    low, high = pl.ds(0, HALF), pl.ds(HALF, HALF)
    halves = (low, high)
    at_end = lax.div(y, 3)
    at_start = lax.div(3 - y, 3)
    inner = at_end + at_start == 0
    t_copies = []
    for h, rows in enumerate(halves):
        slot = 2 + 6 * at_end
        t_copies.append(start(texts.at[0, rows], texts.at[slot, rows], t_send.at[h], t_recv.at[slot, h], ring(2 - 8 * at_end)))
        t_copies.append(start(texts.at[0, rows], texts.at[6, rows], t_send.at[2 + h], t_recv.at[6, h], ring(6)))

    def odd_text(j):
        slot = lax.rem(2 * j + 9 - 2 * k, 8)
        device = ring(1 + 6 * k) if j == 0 else sib
        return start(texts.at[2 * j], texts.at[slot], t_send.at[4 + j], t_recv.at[slot, 0], device)

    t_copies.append(odd_text(0))

    def t_edge(h):
        return remote(texts.at[8, halves[h]], texts.at[2, halves[h]], t_send.at[8 + h], t_recv.at[2, h], ring(8))

    def t_inner(h, slot, n, delta):
        rows = halves[h]
        return remote(texts.at[slot, rows], texts.at[4, rows], t_send.at[n + h], t_recv.at[4, h], ring(delta))

    loads[1].wait()
    loads[2].wait()
    loads[3].wait()
    y_full = jnp.dot(feats[block], proj[...], preferred_element_type=jnp.float32)
    y_full = y_full + rest[...].astype(jnp.float32)
    yv[...] = y_full
    y_sq, image_unit = unit_rows(y_full)
    images[0] = image_unit
    pl.semaphore_wait(reach.at[0], 2)
    tell(1, 2)

    def pair_of(held, a, b):
        return jnp.concatenate([held[a], held[b]], axis=0)

    def gather_grad(unit, pair, first):
        coef = coefficients(unit, pair, scale, bias, first)
        part = jnp.dot(coef, pair, preferred_element_type=jnp.float32)
        if first:
            grad[...] = part
        else:
            grad[...] += part

    for h, rows in enumerate(halves):
        @pl.when(y == 0)
        def _():
            landed(texts.at[8, rows], t_recv.at[8, h])
            t_edge(h).start()

        landed(texts.at[6, rows], t_recv.at[6, h])

        @pl.when(y > 0)
        def _():
            landed(texts.at[2, rows], t_recv.at[2, h])

        @pl.when(inner)
        def _():
            t_inner(h, 6, 10, -2).start()
            t_inner(h, 2, 12, 2).start()

    t_copies.append(odd_text(3))
    pl.semaphore_wait(reach.at[1], 2)
    tell(2, 4)

    def image_copy(n):
        if n == 0:
            slot = 2 + 6 * at_start
            return remote(images.at[0], images.at[slot], i_send.at[0], i_recv.at[slot], ring(8 * at_start - 2))
        return remote(images.at[0], images.at[6], i_send.at[1], i_recv.at[6], ring(-6))

    def odd_image(j):
        slot = lax.rem(2 * j + 7 + 2 * k, 8)
        device = ring(-7 + 6 * k) if j == 0 else sib
        return start(images.at[2 * j], images.at[slot], i_send.at[4 + j], i_recv.at[slot], device)

    image_edge = remote(images.at[8], images.at[2], i_send.at[2], i_recv.at[2], ring(-8))
    image_inner = [
        remote(images.at[6], images.at[4], i_send.at[3], i_recv.at[4], ring(2)),
        remote(images.at[2], images.at[4], i_send.at[8], i_recv.at[4], ring(-2)),
    ]

    @pl.when(jnp.logical_not(inner))
    def _():
        image_copy(0).start()
        image_copy(1).start()

    f_copies = []
    for i in (2, 1, 3):
        f_copies.append(start(feats.at[block], feats.at[block], f_send.at[i], f_recv.at[i], at(xs(i), z, y, k)))
    f_copies.append(start(feats.at[block], feats.at[block], f_send.at[4], f_recv.at[4], sib))

    landed(texts.at[1], t_recv.at[1, 0])
    gather_grad(images[0], pair_of(texts, 0, 1), True)
    landed(texts.at[7], t_recv.at[7, 0])
    gather_grad(images[0], pair_of(texts, 6, 7), False)

    @pl.when(y == 0)
    def _():
        for h, rows in enumerate(halves):
            landed(texts.at[2, rows], t_recv.at[2, h])

    t_copies.append(odd_text(1))
    landed(texts.at[5 - 2 * k], t_recv.at[5 - 2 * k, 0])
    gather_grad(images[0], pair_of(texts, 2, 5 - 2 * k), False)
    for h, rows in enumerate(halves):
        landed(texts.at[4, rows], t_recv.at[4, h])
    t_copies.append(odd_text(2))
    landed(texts.at[3 + 2 * k], t_recv.at[3 + 2 * k, 0])
    gather_grad(images[0], pair_of(texts, 4, 3 + 2 * k), False)

    grad_y = back_norm(yv[...], y_sq, grad[...]).astype(jnp.bfloat16)
    gyt[...] = jnp.transpose(grad_y.astype(jnp.float32)).astype(jnp.bfloat16).reshape(8, ROWS, B)

    x_copies = []
    across = [(2, 0), (2, 1), (1, 0), (1, 1), (3, 0), (3, 1), (0, 1)]
    for n, (i, kk) in enumerate(across):
        other = lax.rem(k + kk, 2)
        x_copies.append(
            start(gyt.at[2 * xs(i) + other], gx.at[block], x_send.at[n], x_recv.at[n], at(xs(i), z, y, other))
        )
    @pl.when(inner)
    def _():
        image_copy(0).start()

    @pl.when(jnp.logical_and(inner, z > 0))
    def _():
        image_copy(1).start()

    gx[block] = gyt[block]
    for i in (1, 3, 2):
        there = feats.at[2 * xs(-i) + k]
        landed(there, f_recv.at[i])
        f_copies.append(start(there, there, f_send.at[4 + i], f_recv.at[4 + i], sib))
    for i in range(4):
        landed(feats.at[2 * xs(-i) + 1 - k], f_recv.at[4 + i])
    for n, (i, kk) in enumerate(across):
        landed(gx.at[2 * xs(-i) + lax.rem(k + kk, 2)], x_recv.at[n])
    left = jnp.concatenate([gx[b] for b in range(8)], axis=1)
    head = jnp.dot(left, feats[...].reshape(8 * B, F), preferred_element_type=jnp.float32)
    for n in range(PARTS * 16):
        i, j = n // 5, n % 5
        if n < TILES:
            tile = head[16 * i : 16 * i + 16, 128 * j : 128 * j + 128]
        else:
            tile = jnp.zeros((16, 128), jnp.float32)
        htf[n // 16, n % 16] = tile
        ht[n // 16, n % 16] = tile.astype(jnp.bfloat16)

    y_copies = []
    for i in (2, 1, 3):
        y_copies.append(
            start(ht.at[:, pl.ds(4 * ys(i), 4)], ry.at[i - 1], y_send.at[i - 1], y_recv.at[i - 1], at(x, z, ys(i), k))
        )
    @pl.when(y == 3)
    def _():
        landed(images.at[8], i_recv.at[8])
        image_edge.start()

    for i in (1, 3, 2):
        landed(ry.at[i - 1], y_recv.at[i - 1])
    mine = htf[:, pl.ds(4 * y, 4)]
    for i in (0, 1, 2):
        mine = mine + ry[i].astype(jnp.float32)
    mine = mine.reshape(OWN, 16, 128)
    sf[...] = mine
    sb[...] = mine.astype(jnp.bfloat16)

    far_first = (8, 7, 9, 6, 10, 5, 11, 4, 12, 3, 13, 2, 14, 1, 15)
    w = lax.rem(z + 12, 16)

    def ws(i):
        return lax.rem(w + (i + 16), 16)

    def z_copy(i):
        return remote(sb.at[ws(i)], rz.at[i - 1], z_send.at[i - 1], z_recv.at[i - 1], at(x, zs(i), y, k))

    pl.semaphore_wait(reach.at[2], 2)
    for i in far_first:
        @pl.when(ws(i) < OWN)
        def _():
            z_copy(i).start()

    @pl.when(jnp.logical_and(inner, z == 0))
    def _():
        image_copy(1).start()

    i_copies = [odd_image(0)]

    part = lax.div(w, 4)
    own = total.at[block, part, 4 * y + lax.rem(w, 4)]

    @pl.when(w < OWN)
    def _():
        for i in range(1, 16):
            landed(rz.at[i - 1], z_recv.at[i - 1])
        tile = sf[w]
        for i in range(15):
            tile = tile + rz[i].astype(jnp.float32)
        own[...] = (tile / N).astype(jnp.bfloat16)

    def a_copy(i):
        return remote(own, own, a_send.at[i - 1], a_recv.at[w], at(x, zs(i), y, k))

    @pl.when(w < OWN)
    def _():
        for i in far_first:
            a_copy(i).start()

    landed(images.at[6], i_recv.at[6])
    landed(images.at[2], i_recv.at[2])

    @pl.when(inner)
    def _():
        for copy in image_inner:
            copy.start()

    i_copies += [odd_image(3), odd_image(1)]
    landed(images.at[1], i_recv.at[1])
    gather_grad(texts[0], pair_of(images, 0, 1), True)
    landed(images.at[7], i_recv.at[7])
    gather_grad(texts[0], pair_of(images, 6, 7), False)
    landed(images.at[3 + 2 * k], i_recv.at[3 + 2 * k])
    gather_grad(texts[0], pair_of(images, 2, 3 + 2 * k), False)

    first = part - lax.div(w, 12)
    last = lax.rem(lax.div(w, 6) + 2, 3)
    b_copies = []
    parts = (first, 3 - first - last, last)
    for n, q in enumerate(parts):
        for r in range(4):
            owner = 4 * q + r

            @pl.when(owner != w)
            def _():
                landed(total.at[block, q, 4 * y + r], a_recv.at[owner])

        there = total.at[block, q, pl.ds(4 * y, 4)]
        for m, (i, j) in enumerate(plane):
            b_copies.append(start(there, there, b_send.at[n, m], b_recv.at[n, m], at(xs(i), z, ys(j), k)))

    landed(images.at[4], i_recv.at[4])
    i_copies.append(odd_image(2))
    landed(images.at[5 - 2 * k], i_recv.at[5 - 2 * k])
    gather_grad(texts[0], pair_of(images, 4, 5 - 2 * k), False)
    gt_ref[...] = back_norm(text[...].astype(jnp.float32), t_sq, grad[...]).astype(jnp.bfloat16)

    c_copies = []
    for n, q in enumerate(parts):
        for i in (0, 1, 3, 2):
            for m, (pi, pj) in enumerate(plane):
                if pi == i:
                    landed(total.at[2 * xs(-pi) + k, q, pl.ds(4 * ys(-pj), 4)], b_recv.at[n, m])
            there = total.at[2 * xs(-i) + k, q]
            c_copies.append(start(there, there, c_send.at[n, i], c_recv.at[n, i], sib))
    for n, q in enumerate(parts):
        for i in (0, 1, 3, 2):
            landed(total.at[2 * xs(-i) + 1 - k, q], c_recv.at[n, i])
    for b in range(8):
        for n in range(TILES):
            i, j = n // 5, n % 5
            headt[ROWS * b + 16 * i : ROWS * b + 16 * i + 16, 128 * j : 128 * j + 128] = total[b, n // 16, n % 16]

    for i in range(9):
        for j in range(5):
            block_t = headt[128 * i : 128 * i + 128, 128 * j : 128 * j + 128].astype(jnp.float32)
            head_ref[128 * j : 128 * j + 128, 128 * i : 128 * i + 128] = jnp.transpose(block_t).astype(jnp.bfloat16)

    for copy in t_copies + f_copies + i_copies + x_copies + y_copies + b_copies + c_copies:
        copy.wait_send()
    for i in far_first:
        @pl.when(ws(i) < OWN)
        def _():
            z_copy(i).wait_send()

    @pl.when(y == 0)
    def _():
        for h in (0, 1):
            t_edge(h).wait_send()

    image_copy(0).wait_send()
    image_copy(1).wait_send()

    @pl.when(y == 3)
    def _():
        image_edge.wait_send()

    @pl.when(inner)
    def _():
        for h in (0, 1):
            t_inner(h, 6, 10, -2).wait_send()
            t_inner(h, 2, 12, 2).wait_send()
        for copy in image_inner:
            copy.wait_send()

    @pl.when(w < OWN)
    def _():
        for i in far_first:
            a_copy(i).wait_send()


def on_device(image_feats, proj_head, rest_part, text_embed, logit_scale, logit_bias):
    any_spec = pl.BlockSpec(memory_space=pl.ANY)
    vmem = pl.BlockSpec(memory_space=pltpu.VMEM)
    smem = pl.BlockSpec(memory_space=pltpu.SMEM)
    bf16, f32 = jnp.bfloat16, jnp.float32
    sems = lambda *n: pltpu.SemaphoreType.DMA(n)
    grad_text, head = pl.pallas_call(
        kernel,
        out_shape=(pltpu.VMEM((B, D), bf16), pltpu.VMEM((F, D), bf16)),
        in_specs=[any_spec] * 4 + [smem] * 2,
        out_specs=(vmem, vmem),
        scratch_shapes=[
            pltpu.VMEM((9, B, D), bf16),
            pltpu.VMEM((9, B, D), bf16),
            pltpu.VMEM((8, B, F), bf16),
            pltpu.VMEM((F, D), bf16),
            pltpu.VMEM((B, D), bf16),
            pltpu.VMEM((B, D), bf16),
            pltpu.VMEM((B, D), f32),
            pltpu.VMEM((B, D), f32),
            pltpu.VMEM((8, ROWS, B), bf16),
            pltpu.VMEM((8, ROWS, B), bf16),
            pltpu.VMEM((PARTS, 16, 16, 128), f32),
            pltpu.VMEM((PARTS, 16, 16, 128), bf16),
            pltpu.VMEM((3, PARTS, 4, 16, 128), bf16),
            pltpu.VMEM((OWN, 16, 128), f32),
            pltpu.VMEM((OWN, 16, 128), bf16),
            pltpu.VMEM((15, 16, 128), bf16),
            pltpu.VMEM((8, PARTS, 16, 16, 128), bf16),
            pltpu.VMEM((D, F), bf16),
            pltpu.SemaphoreType.REGULAR((3,)), sems(4), sems(14), sems(9, 2), sems(9), sems(9), sems(8), sems(8), sems(7), sems(7), sems(3), sems(3),
            sems(15), sems(15), sems(15), sems(12), sems(3, 15), sems(3, 15), sems(3, 4), sems(3, 4),
        ],
        compiler_params=pltpu.CompilerParams(
            collective_id=0, has_side_effects=True, vmem_limit_bytes=60 * 2**20
        ),
    )(image_feats, proj_head, rest_part, text_embed, logit_scale, logit_bias)
    return grad_text, head


def solution(mesh):
    placed = (P("dp", None), P(), P("dp", None), P("dp", None), P(), P())
    return jax.shard_map(
        on_device, mesh=mesh, in_specs=placed, out_specs=(P("dp", None), P()), check_vma=False
    )
```

```python
import jax
import jax.numpy as jnp
from jax import lax
from jax.experimental import pallas as pl
from jax.experimental.pallas import tpu as pltpu
from jax.sharding import PartitionSpec as P

D = 1152
F = 640
B = 128
N = 512
MESH = pl.DeviceIdType.MESH
ROWS = 144
TILES = 45
OWN = 12
PARTS = 3
HALF = B // 2


def unit_rows(values):
    squares = jnp.sum(values * values, axis=-1, keepdims=True) + 1e-06
    return squares, (values / jnp.sqrt(squares)).astype(jnp.bfloat16)


def back_norm(values, squares, grads):
    inner = jnp.sum(values * grads, axis=-1, keepdims=True)
    return (grads - values * (inner / squares)) / jnp.sqrt(squares)


def coefficients(left, right, scale, bias, first):
    logits = bias + scale * lax.dot_general(
        left, right, (((1,), (1,)), ((), ())), preferred_element_type=jnp.float32
    )
    coef = scale * jax.nn.sigmoid(logits)
    if first:
        row = lax.broadcasted_iota(jnp.int32, logits.shape, 0)
        col = lax.broadcasted_iota(jnp.int32, logits.shape, 1)
        coef = jnp.where(row == col, -scale * jax.nn.sigmoid(-logits), coef)
    return coef.astype(jnp.bfloat16)


def kernel(
    feats_hbm, proj_hbm, rest_hbm, text_hbm, scale_ref, bias_ref,
    gt_ref, head_ref,
    texts, images, feats, proj, rest, text, yv, grad, gyt, gx, htf, ht, ry, sf, sb, rz, total, headt,
    reach, load, t_send, t_recv, i_send, i_recv, f_send, f_recv, x_send, x_recv, y_send, y_recv,
    z_send, z_recv, a_send, a_recv, b_send, b_recv, c_send, c_recv,
):
    me = lax.axis_index("dp")
    k = lax.rem(me, 2)
    y = lax.rem(lax.div(me, 2), 4)
    z = lax.rem(lax.div(me, 8), 16)
    x = lax.div(me, 128)
    sib = me + 1 - 2 * k
    block = 2 * x + k

    def ring(delta):
        return lax.rem(me + (delta + N), N)

    def at(ax, az, ay, ak):
        return ((ax * 16 + az) * 4 + ay) * 2 + ak

    def xs(i):
        return lax.rem(x + (i + 4), 4)

    def ys(i):
        return lax.rem(y + (i + 4), 4)

    def zs(i):
        return lax.rem(z + (i + 16), 16)

    def remote(src, dst, send, recv, device):
        return pltpu.make_async_remote_copy(
            src_ref=src, dst_ref=dst, send_sem=send, recv_sem=recv,
            device_id=(device,), device_id_type=MESH,
        )

    def start(*args):
        copy = remote(*args)
        copy.start()
        return copy

    def landed(dst, recv):
        remote(dst, dst, t_send.at[0], recv, sib).wait_recv()

    loads = [
        pltpu.make_async_copy(text_hbm, text, load.at[0]),
        pltpu.make_async_copy(feats_hbm, feats.at[block], load.at[1]),
        pltpu.make_async_copy(proj_hbm, proj, load.at[2]),
        pltpu.make_async_copy(rest_hbm, rest, load.at[3]),
    ]
    for copy in loads:
        copy.start()

    plane = [(2, 2), (2, 1), (2, 3), (1, 2), (3, 2), (1, 1), (1, 3), (3, 1), (3, 3), (0, 2), (2, 0), (1, 0), (3, 0), (0, 1), (0, 3)]
    barrier = pltpu.get_barrier_semaphore()
    partners = [ring(d) for d in (2, -2, 6, -6, 8, -8)] + [sib, ring(-7 + 14 * k)]
    partners += [at(xs(i), z, y, 1 - k) for i in (1, 2, 3)]
    partners += [at(xs(i), z, ys(j), k) for i, j in plane if i == 0 or j == 0]
    partners += [at(x, zs(i), y, k) for i in (1, -1)]
    for device in partners:
        pl.semaphore_signal(barrier, inc=1, device_id=(device,), device_id_type=MESH)

    def tell(n, distance):
        for i in (distance, -distance):
            pl.semaphore_signal(reach.at[n], inc=1, device_id=(at(x, zs(i), y, k),), device_id_type=MESH)

    scale = scale_ref[0]
    bias = bias_ref[0]

    loads[0].wait()
    t_sq, t_unit = unit_rows(text[...].astype(jnp.float32))
    texts[0] = t_unit
    pl.semaphore_wait(barrier, len(partners))
    tell(0, 1)

    low, high = pl.ds(0, HALF), pl.ds(HALF, HALF)
    halves = (low, high)
    at_end = lax.div(y, 3)
    at_start = lax.div(3 - y, 3)
    inner = at_end + at_start == 0
    t_copies = []
    for h, rows in enumerate(halves):
        slot = 2 + 6 * at_end
        t_copies.append(start(texts.at[0, rows], texts.at[6, rows], t_send.at[2 + h], t_recv.at[6, h], ring(6)))
        t_copies.append(start(texts.at[0, rows], texts.at[slot, rows], t_send.at[h], t_recv.at[slot, h], ring(2 - 8 * at_end)))

    def odd_text(j):
        slot = lax.rem(2 * j + 9 - 2 * k, 8)
        device = ring(1 + 6 * k) if j == 0 else sib
        return start(texts.at[2 * j], texts.at[slot], t_send.at[4 + j], t_recv.at[slot, 0], device)

    t_copies.append(odd_text(0))

    def t_edge(h):
        return remote(texts.at[8, halves[h]], texts.at[2, halves[h]], t_send.at[8 + h], t_recv.at[2, h], ring(8))

    def t_inner(h, slot, n, delta):
        rows = halves[h]
        return remote(texts.at[slot, rows], texts.at[4, rows], t_send.at[n + h], t_recv.at[4, h], ring(delta))

    loads[1].wait()
    loads[2].wait()
    loads[3].wait()
    y_full = jnp.dot(feats[block], proj[...], preferred_element_type=jnp.float32)
    y_full = y_full + rest[...].astype(jnp.float32)
    yv[...] = y_full
    y_sq, image_unit = unit_rows(y_full)
    images[0] = image_unit
    pl.semaphore_wait(reach.at[0], 2)
    tell(1, 2)

    def pair_of(held, a, b):
        return jnp.concatenate([held[a], held[b]], axis=0)

    def gather_grad(unit, pair, first):
        coef = coefficients(unit, pair, scale, bias, first)
        part = jnp.dot(coef, pair, preferred_element_type=jnp.float32)
        if first:
            grad[...] = part
        else:
            grad[...] += part

    for h, rows in enumerate(halves):
        @pl.when(y == 0)
        def _():
            landed(texts.at[8, rows], t_recv.at[8, h])
            t_edge(h).start()

        landed(texts.at[6, rows], t_recv.at[6, h])

        @pl.when(y > 0)
        def _():
            landed(texts.at[2, rows], t_recv.at[2, h])

        @pl.when(inner)
        def _():
            t_inner(h, 6, 10, -2).start()
            t_inner(h, 2, 12, 2).start()

    t_copies.append(odd_text(3))
    pl.semaphore_wait(reach.at[1], 2)
    tell(2, 4)

    def image_copy(n):
        if n == 0:
            slot = 2 + 6 * at_start
            return remote(images.at[0], images.at[slot], i_send.at[0], i_recv.at[slot], ring(8 * at_start - 2))
        return remote(images.at[0], images.at[6], i_send.at[1], i_recv.at[6], ring(-6))

    def odd_image(j):
        slot = lax.rem(2 * j + 7 + 2 * k, 8)
        device = ring(-7 + 6 * k) if j == 0 else sib
        return start(images.at[2 * j], images.at[slot], i_send.at[4 + j], i_recv.at[slot], device)

    image_edge = remote(images.at[8], images.at[2], i_send.at[2], i_recv.at[2], ring(-8))
    image_inner = [
        remote(images.at[6], images.at[4], i_send.at[3], i_recv.at[4], ring(2)),
        remote(images.at[2], images.at[4], i_send.at[8], i_recv.at[4], ring(-2)),
    ]

    @pl.when(jnp.logical_not(inner))
    def _():
        image_copy(0).start()
        image_copy(1).start()

    f_copies = []
    for i in (2, 1, 3):
        f_copies.append(start(feats.at[block], feats.at[block], f_send.at[i], f_recv.at[i], at(xs(i), z, y, k)))
    f_copies.append(start(feats.at[block], feats.at[block], f_send.at[4], f_recv.at[4], sib))

    landed(texts.at[1], t_recv.at[1, 0])
    gather_grad(images[0], pair_of(texts, 0, 1), True)
    landed(texts.at[7], t_recv.at[7, 0])
    gather_grad(images[0], pair_of(texts, 6, 7), False)

    @pl.when(y == 0)
    def _():
        for h, rows in enumerate(halves):
            landed(texts.at[2, rows], t_recv.at[2, h])

    t_copies.append(odd_text(1))
    landed(texts.at[5 - 2 * k], t_recv.at[5 - 2 * k, 0])
    gather_grad(images[0], pair_of(texts, 2, 5 - 2 * k), False)
    for h, rows in enumerate(halves):
        landed(texts.at[4, rows], t_recv.at[4, h])
    t_copies.append(odd_text(2))
    landed(texts.at[3 + 2 * k], t_recv.at[3 + 2 * k, 0])
    gather_grad(images[0], pair_of(texts, 4, 3 + 2 * k), False)

    grad_y = back_norm(yv[...], y_sq, grad[...]).astype(jnp.bfloat16)
    gyt[...] = jnp.transpose(grad_y.astype(jnp.float32)).astype(jnp.bfloat16).reshape(8, ROWS, B)

    x_copies = []
    across = [(2, 0), (2, 1), (1, 0), (1, 1), (3, 0), (3, 1), (0, 1)]
    for n, (i, kk) in enumerate(across):
        other = lax.rem(k + kk, 2)
        x_copies.append(
            start(gyt.at[2 * xs(i) + other], gx.at[block], x_send.at[n], x_recv.at[n], at(xs(i), z, y, other))
        )
    @pl.when(inner)
    def _():
        image_copy(0).start()

    @pl.when(jnp.logical_and(inner, z > 0))
    def _():
        image_copy(1).start()

    gx[block] = gyt[block]
    for i in (1, 3, 2):
        there = feats.at[2 * xs(-i) + k]
        landed(there, f_recv.at[i])
        f_copies.append(start(there, there, f_send.at[4 + i], f_recv.at[4 + i], sib))
    for i in range(4):
        landed(feats.at[2 * xs(-i) + 1 - k], f_recv.at[4 + i])
    for n, (i, kk) in enumerate(across):
        landed(gx.at[2 * xs(-i) + lax.rem(k + kk, 2)], x_recv.at[n])
    left = jnp.concatenate([gx[b] for b in range(8)], axis=1)
    head = jnp.dot(left, feats[...].reshape(8 * B, F), preferred_element_type=jnp.float32)
    for n in range(PARTS * 16):
        i, j = n // 5, n % 5
        if n < TILES:
            tile = head[16 * i : 16 * i + 16, 128 * j : 128 * j + 128]
        else:
            tile = jnp.zeros((16, 128), jnp.float32)
        htf[n // 16, n % 16] = tile
        ht[n // 16, n % 16] = tile.astype(jnp.bfloat16)

    y_copies = []
    for i in (2, 1, 3):
        y_copies.append(
            start(ht.at[:, pl.ds(4 * ys(i), 4)], ry.at[i - 1], y_send.at[i - 1], y_recv.at[i - 1], at(x, z, ys(i), k))
        )
    @pl.when(y == 3)
    def _():
        landed(images.at[8], i_recv.at[8])
        image_edge.start()

    for i in (1, 3, 2):
        landed(ry.at[i - 1], y_recv.at[i - 1])
    mine = htf[:, pl.ds(4 * y, 4)]
    for i in (0, 1, 2):
        mine = mine + ry[i].astype(jnp.float32)
    mine = mine.reshape(OWN, 16, 128)
    sf[...] = mine
    sb[...] = mine.astype(jnp.bfloat16)

    far_first = (8, 7, 9, 6, 10, 5, 11, 4, 12, 3, 13, 2, 14, 1, 15)
    w = lax.rem(z + 12, 16)

    def ws(i):
        return lax.rem(w + (i + 16), 16)

    def z_copy(i):
        return remote(sb.at[ws(i)], rz.at[i - 1], z_send.at[i - 1], z_recv.at[i - 1], at(x, zs(i), y, k))

    pl.semaphore_wait(reach.at[2], 2)
    for i in far_first:
        @pl.when(ws(i) < OWN)
        def _():
            z_copy(i).start()

    @pl.when(jnp.logical_and(inner, z == 0))
    def _():
        image_copy(1).start()

    i_copies = [odd_image(0)]

    part = lax.div(w, 4)
    own = total.at[block, part, 4 * y + lax.rem(w, 4)]

    @pl.when(w < OWN)
    def _():
        for i in range(1, 16):
            landed(rz.at[i - 1], z_recv.at[i - 1])
        tile = sf[w]
        for i in range(15):
            tile = tile + rz[i].astype(jnp.float32)
        own[...] = (tile / N).astype(jnp.bfloat16)

    def a_copy(i):
        return remote(own, own, a_send.at[i - 1], a_recv.at[w], at(x, zs(i), y, k))

    @pl.when(w < OWN)
    def _():
        for i in far_first:
            a_copy(i).start()

    landed(images.at[6], i_recv.at[6])
    landed(images.at[2], i_recv.at[2])

    @pl.when(inner)
    def _():
        for copy in image_inner:
            copy.start()

    i_copies += [odd_image(3), odd_image(1)]
    landed(images.at[1], i_recv.at[1])
    gather_grad(texts[0], pair_of(images, 0, 1), True)
    landed(images.at[7], i_recv.at[7])
    gather_grad(texts[0], pair_of(images, 6, 7), False)
    landed(images.at[3 + 2 * k], i_recv.at[3 + 2 * k])
    gather_grad(texts[0], pair_of(images, 2, 3 + 2 * k), False)

    first = part - lax.div(w, 12)
    last = lax.rem(lax.div(w, 6) + 2, 3)
    b_copies = []
    parts = (first, 3 - first - last, last)
    for n, q in enumerate(parts):
        for r in range(4):
            owner = 4 * q + r

            @pl.when(owner != w)
            def _():
                landed(total.at[block, q, 4 * y + r], a_recv.at[owner])

        there = total.at[block, q, pl.ds(4 * y, 4)]
        for m, (i, j) in enumerate(plane):
            b_copies.append(start(there, there, b_send.at[n, m], b_recv.at[n, m], at(xs(i), z, ys(j), k)))

    landed(images.at[4], i_recv.at[4])
    i_copies.append(odd_image(2))
    landed(images.at[5 - 2 * k], i_recv.at[5 - 2 * k])
    gather_grad(texts[0], pair_of(images, 4, 5 - 2 * k), False)
    gt_ref[...] = back_norm(text[...].astype(jnp.float32), t_sq, grad[...]).astype(jnp.bfloat16)

    c_copies = []
    for n, q in enumerate(parts):
        for i in (0, 1, 3, 2):
            for m, (pi, pj) in enumerate(plane):
                if pi == i:
                    landed(total.at[2 * xs(-pi) + k, q, pl.ds(4 * ys(-pj), 4)], b_recv.at[n, m])
            there = total.at[2 * xs(-i) + k, q]
            c_copies.append(start(there, there, c_send.at[n, i], c_recv.at[n, i], sib))
    def assemble(b):
        base = pl.multiple_of(ROWS * b, 16)
        for n in range(TILES):
            i, j = n // 5, n % 5
            headt[pl.ds(base + 16 * i, 16), 128 * j : 128 * j + 128] = total[b, n // 16, n % 16]

    for i in (0, 1, 3, 2):
        assemble(2 * xs(-i) + k)
    for n, q in enumerate(parts):
        for i in (0, 1, 3, 2):
            landed(total.at[2 * xs(-i) + 1 - k, q], c_recv.at[n, i])
    for i in (0, 1, 3, 2):
        assemble(2 * xs(-i) + 1 - k)
    for i in range(9):
        for j in range(5):
            block_t = headt[128 * i : 128 * i + 128, 128 * j : 128 * j + 128].astype(jnp.float32)
            head_ref[128 * j : 128 * j + 128, 128 * i : 128 * i + 128] = jnp.transpose(block_t).astype(jnp.bfloat16)

    for copy in t_copies + f_copies + i_copies + x_copies + y_copies + b_copies + c_copies:
        copy.wait_send()
    for i in far_first:
        @pl.when(ws(i) < OWN)
        def _():
            z_copy(i).wait_send()

    @pl.when(y == 0)
    def _():
        for h in (0, 1):
            t_edge(h).wait_send()

    image_copy(0).wait_send()
    image_copy(1).wait_send()

    @pl.when(y == 3)
    def _():
        image_edge.wait_send()

    @pl.when(inner)
    def _():
        for h in (0, 1):
            t_inner(h, 6, 10, -2).wait_send()
            t_inner(h, 2, 12, 2).wait_send()
        for copy in image_inner:
            copy.wait_send()

    @pl.when(w < OWN)
    def _():
        for i in far_first:
            a_copy(i).wait_send()


def on_device(image_feats, proj_head, rest_part, text_embed, logit_scale, logit_bias):
    any_spec = pl.BlockSpec(memory_space=pl.ANY)
    vmem = pl.BlockSpec(memory_space=pltpu.VMEM)
    smem = pl.BlockSpec(memory_space=pltpu.SMEM)
    bf16, f32 = jnp.bfloat16, jnp.float32
    sems = lambda *n: pltpu.SemaphoreType.DMA(n)
    grad_text, head = pl.pallas_call(
        kernel,
        out_shape=(pltpu.VMEM((B, D), bf16), pltpu.VMEM((F, D), bf16)),
        in_specs=[any_spec] * 4 + [smem] * 2,
        out_specs=(vmem, vmem),
        scratch_shapes=[
            pltpu.VMEM((9, B, D), bf16),
            pltpu.VMEM((9, B, D), bf16),
            pltpu.VMEM((8, B, F), bf16),
            pltpu.VMEM((F, D), bf16),
            pltpu.VMEM((B, D), bf16),
            pltpu.VMEM((B, D), bf16),
            pltpu.VMEM((B, D), f32),
            pltpu.VMEM((B, D), f32),
            pltpu.VMEM((8, ROWS, B), bf16),
            pltpu.VMEM((8, ROWS, B), bf16),
            pltpu.VMEM((PARTS, 16, 16, 128), f32),
            pltpu.VMEM((PARTS, 16, 16, 128), bf16),
            pltpu.VMEM((3, PARTS, 4, 16, 128), bf16),
            pltpu.VMEM((OWN, 16, 128), f32),
            pltpu.VMEM((OWN, 16, 128), bf16),
            pltpu.VMEM((15, 16, 128), bf16),
            pltpu.VMEM((8, PARTS, 16, 16, 128), bf16),
            pltpu.VMEM((D, F), bf16),
            pltpu.SemaphoreType.REGULAR((3,)), sems(4), sems(14), sems(9, 2), sems(9), sems(9), sems(8), sems(8), sems(7), sems(7), sems(3), sems(3),
            sems(15), sems(15), sems(15), sems(12), sems(3, 15), sems(3, 15), sems(3, 4), sems(3, 4),
        ],
        compiler_params=pltpu.CompilerParams(
            collective_id=0, has_side_effects=True, vmem_limit_bytes=60 * 2**20
        ),
    )(image_feats, proj_head, rest_part, text_embed, logit_scale, logit_bias)
    return grad_text, head


def solution(mesh):
    placed = (P("dp", None), P(), P("dp", None), P("dp", None), P(), P())
    return jax.shard_map(
        on_device, mesh=mesh, in_specs=placed, out_specs=(P("dp", None), P()), check_vma=False
    )
```
